32 devices in a mesh: row: 4 (over z), col: 4 (over x, core), depth: 2 (over y).
Axes of the slice: x: 2, y: 2, z: 4, core: 2. Of those that a mesh axis runs over, the one named last changes fastest.
Arguments:
- intersection_re: bfloat16 [2, 4096, 4096], P('depth', ('row', 'col')), may hold values from -1 to 1, as said below
- intersection_im: bfloat16 [2, 4096, 4096], P('depth', ('row', 'col')), may hold values from -1 to 1, as said below
- weights: float32 [2], replicated, may hold values from 0.5 to 2
- shells: int32 [2, 3], replicated, may hold values from -2 to 2
- rotation: bfloat16 [4096, 4096], P(('row', 'col')), may hold values from -6 to 6
Outputs:
- updated: float32 [4096, 4096], P(('row', 'col'), 'depth')
The draws below stay inside these ranges and needn't reach their ends.
Inputs may be any that keep to these rules, and one draw needn't show every extreme that they name: `intersection_re`: diagonal entries lie in 0.5 to 1. `intersection_im`: diagonal entries lie in -0.6 to 0.6.
All inputs are finite; a program needn't handle non-finite values.
Results may differ from the reference program's by a relative error of at most 0.035.
Values may be sent and summed in bfloat16 or wider, within the bound.
A program may use at most 64 MiB of HBM per device.

```python
import math
import jax
import jax.numpy as jnp

WF = 4096
TERMS = 8
B = 2


def intersection_common(key, diag_lo, diag_hi):
    base_key, diag_key = jax.random.split(key, 2)
    values = jax.random.normal(base_key, (B, WF, WF), jnp.float32)
    values = values * WF ** (-0.5)
    diagonal = jax.random.uniform(diag_key, (B, WF), jnp.float32, diag_lo, diag_hi)
    index = jnp.arange(WF)
    values = values.at[:, index, index].set(diagonal)
    return values.astype(jnp.bfloat16)


def draw_intersection_re(key, part):
    return intersection_common(jax.random.fold_in(key, 11), 0.5, 1.0)


def draw_intersection_im(key, part):
    return intersection_common(jax.random.fold_in(key, 23), -0.6, 0.6)


def plant(entries, own_key, least, high):
    dims = entries.shape
    index_at = [jax.random.randint(jax.random.fold_in(own_key, axis), (), 0, dims[axis]) for axis in range(len(dims))]
    entries = entries.at[tuple(index_at)].set(least)
    longest = dims.index(max(dims))
    index_at[longest] = (index_at[longest] + 1) % dims[longest]
    return entries.at[tuple(index_at)].set(high)


def level_of(stream_key, shape, cuts, least, high):
    def one(axis_at, shards_of):
        draws = jax.random.uniform(jax.random.fold_in(jax.random.fold_in(stream_key, 6), axis_at), (shards_of,), jnp.float32, least / len(cuts), high / len(cuts))
        return jnp.repeat(jnp.exp(draws), shape[axis_at] // shards_of).reshape((-1,) + (1,) * (len(shape) - axis_at - 1))

    factor_of = one(*cuts[0])
    for cut in cuts[1:]:
        factor_of = factor_of * one(*cut)
    return factor_of


def noise(rng, shape, deviation, bound, shards=(), dtype=jnp.bfloat16):
    entries = deviation * jax.random.normal(rng, shape, jnp.float32)
    if shards:
        entries = entries * level_of(rng, shape, shards, -0.22, 0.18)
    return jnp.clip(entries, -bound, bound).astype(dtype)


def setup_inputs(seed: int = 0) -> dict:
    key_list = jax.random.split(jax.random.key(seed), 6)
    return {
        "intersection_re": draw_intersection_re(jax.random.fold_in(key_list[5], 71), 0),
        "intersection_im": draw_intersection_im(jax.random.fold_in(key_list[5], 71), 0),
        "weights": jnp.clip(jnp.exp(jax.random.uniform(key_list[2], (B,), jnp.float32, math.log(0.5), math.log(2.0))), 0.5, 2.0),
        "shells": plant(jax.random.randint(key_list[3], (B, 3), -2, 3), jax.random.fold_in(key_list[3], 1), -2, 2).astype(jnp.int32),
        "rotation": noise(key_list[4], (WF, WF), 0.5, 6.0, ((0, 16),)),
    }


LATTICE = 0.25

def reference(intersection_re, intersection_im, weights, shells, rotation):
    index = jnp.arange(WF)
    diag_re = intersection_re[:, index, index].astype(jnp.float32)
    diag_im = intersection_im[:, index, index].astype(jnp.float32)
    phase = jnp.arctan2(diag_im, diag_re)
    vectors = shells.astype(jnp.float32) * LATTICE
    centre = -jnp.einsum('bk,bn->kn', weights[:, None] * vectors, phase)
    spread = phase + jnp.einsum('bk,kn->bn', vectors, centre)
    modulus = diag_re * diag_re + diag_im * diag_im
    summed = jnp.zeros((WF, WF), jnp.float32)
    for shell in range(B):
        values_re = intersection_re[shell].astype(jnp.float32)
        values_im = intersection_im[shell].astype(jnp.float32)
        terms = values_re * diag_re[shell][None, :] + values_im * diag_im[shell][None, :]
        terms = terms - spread[shell][None, :] * (values_im * diag_re[shell][None, :] - values_re * diag_im[shell][None, :]) / modulus[shell][None, :]
        summed = summed + weights[shell] * terms
    factor = 1.25 / math.sqrt(B)
    generator = ((summed - summed.T) * factor).astype(jnp.bfloat16)
    series_term = rotation
    accum = rotation.astype(jnp.float32)
    for order in range(1, TERMS):
        product = jnp.dot(series_term, generator, preferred_element_type=jnp.float32)
        series_term = (product / order).astype(jnp.bfloat16)
        accum = accum + series_term.astype(jnp.float32)
    return accum
```

```python
import functools
import math

import jax
import jax.numpy as jnp
from jax import lax
from jax.experimental import pallas as pl
from jax.experimental.pallas import tpu as pltpu
from jax.sharding import PartitionSpec as P

TERMS = 8


LATTICE = 0.25


def shift(at, axis, way):
    z, x, y, core = at
    if axis == "z":
        return (z + way, x, y, core)
    if axis == "x":
        return (z, 1 - x, y, core)
    if axis == "y":
        return (z, x, 1 - y, core)
    return (z, x, y, 1 - core)


def device_of(at):
    z, x, y, core = at
    return {"row": z, "col": x * 2 + core, "depth": y}


ORDERS = (("z", "x", "y"), ("x", "y", "z"), ("y", "z", "x"))


def cut(width, parts):
    unit = width // 128
    ends = [unit * i // parts * 128 for i in range(parts + 1)]
    return [(ends[i], ends[i + 1] - ends[i]) for i in range(parts)]


def series_kernel(
    rows_count, piece_ref, rotation_ref, out_ref,
    gen, term, accum, sent, got,
    own_sem, link_sem, side_sem, send_sem, last_send, last_recv,
):
    z = lax.axis_index("row")
    col = lax.axis_index("col")
    y = lax.axis_index("depth")
    x = col // 2
    core = col % 2
    me = (z, x, y, core)
    rows, width = piece_ref.shape
    segments = cut(width, len(ORDERS))

    def exists(axis, way):
        if axis != "z":
            return None
        return z > 0 if way < 0 else z < rows_count - 1

    def guarded(condition, action):
        if condition is None:
            action()
        else:
            pl.when(condition)(action)

    barrier = pltpu.get_barrier_semaphore()
    moves = [("z", -1), ("z", 1), ("x", 1), ("y", 1), ("core", 1)]
    for axis, way in moves:
        def greet(axis=axis, way=way):
            pl.semaphore_signal(
                barrier, inc=1, device_id=device_of(shift(me, axis, way)),
                device_id_type=pl.DeviceIdType.MESH,
            )
        guarded(exists(axis, way), greet)
    peers = 3 + jnp.where(z > 0, 1, 0) + jnp.where(z < rows_count - 1, 1, 0)
    pl.semaphore_wait(barrier, peers)

    def slab(at):
        zo, xo, yo, co = at
        return ((zo * 2 + xo) * 2 + co) * 2 + yo

    own = pltpu.make_async_copy(
        piece_ref, gen.at[pl.ds(pl.multiple_of(slab(me) * rows, rows), rows), :], own_sem
    )
    own.start()
    own.wait()

    def copy(seg, origin, move, recv):
        start, size = segments[seg]
        place = gen.at[
            pl.ds(pl.multiple_of(slab(origin) * rows, rows), rows), pl.ds(start, size)
        ]
        axis, way = move
        return pltpu.make_async_remote_copy(
            src_ref=place, dst_ref=place,
            send_sem=send_sem.at[seg, moves.index(move), slab(origin) % (rows_count * 8)],
            recv_sem=recv.at[seg, slab(origin)],
            device_id=device_of(shift(me, axis, way)),
            device_id_type=pl.DeviceIdType.MESH,
        )

    plan = []
    for dz in range(1 - rows_count, rows_count):
        for dx in range(2):
            for dy in range(2):
                for seg, order in enumerate(ORDERS):
                    offset = {"z": dz, "x": dx, "y": dy}
                    last = max([i for i, a in enumerate(order) if offset[a]], default=-1)
                    onward = []
                    if last >= 0 and order[last] == "z":
                        onward.append(("z", 1 if dz < 0 else -1))
                    for axis in order[last + 1:]:
                        onward += [("z", -1), ("z", 1)] if axis == "z" else [(axis, 1)]
                    plan.append((abs(dz) + dx + dy, seg, dz, dx, dy, onward))
    plan.sort(key=lambda entry: entry[:2])

    def origin_of(dz, dx, dy):
        return (z + dz, 1 - x if dx else x, 1 - y if dy else y, core)

    def inside(dz):
        if dz == 0:
            return None
        return z + dz >= 0 if dz < 0 else z + dz < rows_count

    for hops, seg, dz, dx, dy, onward in plan:
        def handle(hops=hops, seg=seg, dz=dz, dx=dx, dy=dy, onward=onward):
            origin = origin_of(dz, dx, dy)
            if hops:
                copy(seg, origin, ("x", 1), link_sem).wait_recv()
            for move in onward:
                guarded(exists(*move), lambda move=move: copy(seg, origin, move, link_sem).start())
            copy(seg, origin, ("core", 1), side_sem).start()
        guarded(inside(dz), handle)

    for seg in range(len(ORDERS)):
        for zo in range(rows_count):
            for xo in range(2):
                for yo in range(2):
                    copy(seg, (zo, xo, yo, 1 - core), ("core", 1), side_sem).wait_recv()

    chunk = 512
    half = width // 2
    other = device_of(shift(me, "y", 1))

    def last_copy(index):
        place = pl.ds(index * chunk, chunk)
        return pltpu.make_async_remote_copy(
            src_ref=sent.at[:, place], dst_ref=got.at[:, place],
            send_sem=last_send.at[index], recv_sem=last_recv.at[index],
            device_id=other, device_id_type=pl.DeviceIdType.MESH,
        )

    own_rows = pl.ds(pl.multiple_of(y * rows, rows), rows)
    other_rows = pl.ds(pl.multiple_of((1 - y) * rows, rows), rows)
    for order in range(1, TERMS):
        source = rotation_ref if order == 1 else term.at[(order - 1) % 2]

        def product(place):
            value = jnp.dot(source[...], gen[:, place], preferred_element_type=jnp.float32)
            return (value * (1.0 / order)).astype(jnp.bfloat16)

        if order + 1 < TERMS:
            @pl.loop(0, width // chunk)
            def _(index):
                place = pl.ds(pl.multiple_of(index * chunk, chunk), chunk)
                value = product(place)
                term[order % 2, :, place] = value
                base = rotation_ref[:, place].astype(jnp.float32) if order == 1 else accum[:, place]
                accum[:, place] = base + value.astype(jnp.float32)
        else:
            for index in range(half // chunk):
                place = pl.ds(pl.multiple_of((1 - y) * half + index * chunk, chunk), chunk)
                total = accum[:, place] + product(place).astype(jnp.float32)
                sent[:, index * chunk:(index + 1) * chunk] = total.astype(jnp.bfloat16)
                last_copy(index).start()
            for index in range(half // chunk):
                place = pl.ds(pl.multiple_of(y * half + index * chunk, chunk), chunk)
                total = accum[:, place] + product(place).astype(jnp.float32)
                out_ref[own_rows, index * chunk:(index + 1) * chunk] = total
    for index in range(half // chunk):
        last_copy(index).wait_recv()
        part = slice(index * chunk, (index + 1) * chunk)
        out_ref[other_rows, part] = got[:, part].astype(jnp.float32)
    for index in range(half // chunk):
        last_copy(index).wait_send()
    for hops, seg, dz, dx, dy, onward in plan:
        def finish(seg=seg, dz=dz, dx=dx, dy=dy, onward=onward):
            origin = origin_of(dz, dx, dy)
            for move in onward:
                guarded(exists(*move), lambda move=move: copy(seg, origin, move, link_sem).wait_send())
            copy(seg, origin, ("core", 1), side_sem).wait_send()
        guarded(inside(dz), finish)


def series(rows_count, piece, rotation_piece):
    rows, width = piece.shape
    pieces = rows_count * 8
    segs = len(ORDERS)
    vmem = pl.BlockSpec(memory_space=pltpu.VMEM)
    return pl.pallas_call(
        functools.partial(series_kernel, rows_count),
        out_shape=jax.ShapeDtypeStruct((2 * rows, width // 2), jnp.float32),
        in_specs=[vmem, vmem],
        out_specs=vmem,
        scratch_shapes=[
            pltpu.VMEM((width, width), jnp.bfloat16),
            pltpu.VMEM((2, rows, width), jnp.bfloat16),
            pltpu.VMEM((rows, width), jnp.float32),
            pltpu.VMEM((rows, width // 2), jnp.bfloat16),
            pltpu.VMEM((rows, width // 2), jnp.bfloat16),
            pltpu.SemaphoreType.DMA,
            pltpu.SemaphoreType.DMA((segs, pieces)),
            pltpu.SemaphoreType.DMA((segs, pieces)),
            pltpu.SemaphoreType.DMA((segs, 5, pieces)),
            pltpu.SemaphoreType.DMA((width // 1024,)),
            pltpu.SemaphoreType.DMA((width // 1024,)),
        ],
        compiler_params=pltpu.CompilerParams(
            collective_id=3, has_side_effects=True, vmem_limit_bytes=50 * 2**20
        ),
    )(piece, rotation_piece)


def per_device(rows_count, fast, intersection_re, intersection_im, weights, shells, rotation):
    shells_here = intersection_re.shape[0]
    slab_rows = intersection_re.shape[1]
    width = intersection_re.shape[2]
    position = lax.axis_index(("row", "col"))
    layer_index = lax.axis_index("depth")
    depth_count = lax.axis_size("depth")
    block_re = lax.dynamic_slice_in_dim(intersection_re, position * slab_rows, slab_rows, 2)
    block_im = lax.dynamic_slice_in_dim(intersection_im, position * slab_rows, slab_rows, 2)
    diag_piece = jnp.stack(
        [jnp.diagonal(block_re, axis1=1, axis2=2), jnp.diagonal(block_im, axis1=1, axis2=2)], 1
    )
    first_shell = layer_index * shells_here
    own_weights = lax.dynamic_slice_in_dim(weights, first_shell, shells_here, 0)
    own_vectors = (
        lax.dynamic_slice_in_dim(shells, first_shell, shells_here, 0).astype(jnp.float32) * LATTICE
    )
    diagonals = lax.all_gather(diag_piece, ("row", "col"), axis=2, tiled=True).astype(jnp.float32)
    diag_re = diagonals[:, 0]
    diag_im = diagonals[:, 1]
    phase_own = jnp.arctan2(diag_im, diag_re)
    partial_centre = -jnp.einsum("bk,bn->kn", own_weights[:, None] * own_vectors, phase_own)
    centre = lax.psum(partial_centre, "depth")
    spread = phase_own + jnp.einsum("bk,kn->bn", own_vectors, centre)
    modulus = diag_re * diag_re + diag_im * diag_im
    values_re = intersection_re.astype(jnp.float32)
    values_im = intersection_im.astype(jnp.float32)
    terms = values_re * diag_re[:, None, :] + values_im * diag_im[:, None, :]
    terms = (
        terms
        - spread[:, None, :]
        * (values_im * diag_re[:, None, :] - values_re * diag_im[:, None, :])
        / modulus[:, None, :]
    )
    local_sum = jnp.sum(own_weights[:, None, None] * terms, 0)
    factor = 1.25 / math.sqrt(depth_count * shells_here)
    slab_cols = width // depth_count
    if fast:
        narrow = local_sum.astype(jnp.bfloat16)
        mirrored = lax.all_to_all(narrow, ("row", "col"), split_axis=1, concat_axis=0, tiled=True)
        anti = (local_sum - mirrored.T.astype(jnp.float32)) * factor
        piece = lax.psum_scatter(
            anti.astype(jnp.bfloat16), "depth", scatter_dimension=0, tiled=True
        )
        part = slab_rows // depth_count
        own_rotation = lax.dynamic_slice_in_dim(rotation, layer_index * part, part, 0)
        return series(rows_count, piece, own_rotation)
    mirrored = lax.all_to_all(local_sum, ("row", "col"), split_axis=1, concat_axis=0, tiled=True).T
    operator_rows = (
        lax.psum_scatter(local_sum - mirrored, "depth", scatter_dimension=1, tiled=True) * factor
    )
    operator_piece = operator_rows.astype(jnp.bfloat16)
    operator_cols = lax.all_gather(operator_piece, ("row", "col"), axis=0, tiled=True)
    accum = lax.dynamic_slice_in_dim(rotation, layer_index * slab_cols, slab_cols, 1).astype(
        jnp.float32
    )
    product = jnp.dot(rotation, operator_cols, preferred_element_type=jnp.float32)
    for order in range(1, TERMS):
        series_term = (product / order).astype(jnp.bfloat16)
        accum = accum + series_term.astype(jnp.float32)
        if order + 1 < TERMS:
            piece = lax.all_gather(series_term, "depth", axis=1, tiled=True)
            matching = lax.slice_in_dim(operator_cols, 0, piece.shape[1], axis=0)
            product = jnp.zeros_like(accum) + jnp.dot(
                piece, matching, preferred_element_type=jnp.float32
            )
    return accum


def solution(mesh):
    in_specs = (
        P("depth", ("row", "col"), None),
        P("depth", ("row", "col"), None),
        P(),
        P(),
        P(("row", "col"), None),
    )
    out_specs = P(("row", "col"), "depth")
    rows_count = mesh.shape["row"]
    fast = mesh.shape["col"] == 4 and mesh.shape["depth"] == 2
    return jax.shard_map(
        functools.partial(per_device, rows_count, fast), mesh=mesh, in_specs=in_specs, out_specs=out_specs, check_vma=False
    )
```

```python
import functools
import math

import jax
import jax.numpy as jnp
from jax import lax
from jax.experimental import pallas as pl
from jax.experimental.pallas import tpu as pltpu
from jax.sharding import PartitionSpec as P

TERMS = 8


LATTICE = 0.25


def shift(at, axis, way):
    z, x, y, core = at
    if axis == "z":
        return (z + way, x, y, core)
    if axis == "x":
        return (z, 1 - x, y, core)
    if axis == "y":
        return (z, x, 1 - y, core)
    return (z, x, y, 1 - core)


def device_of(at):
    z, x, y, core = at
    return {"row": z, "col": x * 2 + core, "depth": y}


ORDERS = (("z", "x", "y"), ("x", "y", "z"), ("y", "z", "x"))


def cut(width, parts):
    unit = width // 128
    ends = [unit * i // parts * 128 for i in range(parts + 1)]
    return [(ends[i], ends[i + 1] - ends[i]) for i in range(parts)]


def series_kernel(
    rows_count, piece_ref, rotation_ref, out_ref,
    gen, term, accum, sent, got,
    own_sem, link_sem, side_sem, send_sem, last_send, last_recv,
):
    z = lax.axis_index("row")
    col = lax.axis_index("col")
    y = lax.axis_index("depth")
    x = col // 2
    core = col % 2
    me = (z, x, y, core)
    rows, width = piece_ref.shape
    segments = cut(width, len(ORDERS))

    def exists(axis, way):
        if axis != "z":
            return None
        return z > 0 if way < 0 else z < rows_count - 1

    def guarded(condition, action):
        if condition is None:
            action()
        else:
            pl.when(condition)(action)

    barrier = pltpu.get_barrier_semaphore()
    moves = [("z", -1), ("z", 1), ("x", 1), ("y", 1), ("core", 1)]
    for axis, way in moves:
        def greet(axis=axis, way=way):
            pl.semaphore_signal(
                barrier, inc=1, device_id=device_of(shift(me, axis, way)),
                device_id_type=pl.DeviceIdType.MESH,
            )
        guarded(exists(axis, way), greet)
    peers = 3 + jnp.where(z > 0, 1, 0) + jnp.where(z < rows_count - 1, 1, 0)
    pl.semaphore_wait(barrier, peers)

    def slab(at):
        zo, xo, yo, co = at
        return ((zo * 2 + xo) * 2 + co) * 2 + yo

    own = pltpu.make_async_copy(
        piece_ref, gen.at[pl.ds(pl.multiple_of(slab(me) * rows, rows), rows), :], own_sem
    )
    own.start()
    own.wait()

    def copy(seg, origin, move, recv):
        start, size = segments[seg]
        place = gen.at[
            pl.ds(pl.multiple_of(slab(origin) * rows, rows), rows), pl.ds(start, size)
        ]
        axis, way = move
        return pltpu.make_async_remote_copy(
            src_ref=place, dst_ref=place,
            send_sem=send_sem.at[seg, moves.index(move), slab(origin) % (rows_count * 8)],
            recv_sem=recv.at[seg, slab(origin)],
            device_id=device_of(shift(me, axis, way)),
            device_id_type=pl.DeviceIdType.MESH,
        )

    plan = []
    for dz in range(1 - rows_count, rows_count):
        for dx in range(2):
            for dy in range(2):
                for seg, order in enumerate(ORDERS):
                    offset = {"z": dz, "x": dx, "y": dy}
                    last = max([i for i, a in enumerate(order) if offset[a]], default=-1)
                    onward = []
                    if last >= 0 and order[last] == "z":
                        onward.append(("z", 1 if dz < 0 else -1))
                    for axis in order[last + 1:]:
                        onward += [("z", -1), ("z", 1)] if axis == "z" else [(axis, 1)]
                    plan.append((abs(dz) + dx + dy, seg, dz, dx, dy, onward))
    plan.sort(key=lambda entry: entry[:2])

    def origin_of(dz, dx, dy):
        return (z + dz, 1 - x if dx else x, 1 - y if dy else y, core)

    def inside(dz):
        if dz == 0:
            return None
        return z + dz >= 0 if dz < 0 else z + dz < rows_count

    for hops, seg, dz, dx, dy, onward in plan:
        def handle(hops=hops, seg=seg, dz=dz, dx=dx, dy=dy, onward=onward):
            origin = origin_of(dz, dx, dy)
            if hops:
                copy(seg, origin, ("x", 1), link_sem).wait_recv()
            for move in onward:
                guarded(exists(*move), lambda move=move: copy(seg, origin, move, link_sem).start())
            copy(seg, origin, ("core", 1), side_sem).start()
        guarded(inside(dz), handle)

    for seg in range(len(ORDERS)):
        for zo in range(rows_count):
            for xo in range(2):
                for yo in range(2):
                    copy(seg, (zo, xo, yo, 1 - core), ("core", 1), side_sem).wait_recv()

    chunk = 512
    half = width // 2
    other = device_of(shift(me, "y", 1))

    def last_copy(index):
        place = pl.ds(index * chunk, chunk)
        return pltpu.make_async_remote_copy(
            src_ref=sent.at[:, place], dst_ref=got.at[:, place],
            send_sem=last_send.at[index], recv_sem=last_recv.at[index],
            device_id=other, device_id_type=pl.DeviceIdType.MESH,
        )

    own_rows = pl.ds(pl.multiple_of(y * rows, rows), rows)
    other_rows = pl.ds(pl.multiple_of((1 - y) * rows, rows), rows)
    for order in range(1, TERMS):
        source = rotation_ref if order == 1 else term.at[(order - 1) % 2]

        def product(place):
            value = jnp.dot(source[...], gen[:, place], preferred_element_type=jnp.float32)
            return (value * (1.0 / order)).astype(jnp.bfloat16)

        if order + 1 < TERMS:
            @pl.loop(0, width // chunk)
            def _(index):
                place = pl.ds(pl.multiple_of(index * chunk, chunk), chunk)
                value = product(place)
                term[order % 2, :, place] = value
                base = rotation_ref[:, place].astype(jnp.float32) if order == 1 else accum[:, place]
                accum[:, place] = base + value.astype(jnp.float32)
        else:
            for index in range(half // chunk):
                place = pl.ds(pl.multiple_of((1 - y) * half + index * chunk, chunk), chunk)
                total = accum[:, place] + product(place).astype(jnp.float32)
                sent[:, index * chunk:(index + 1) * chunk] = total.astype(jnp.bfloat16)
                last_copy(index).start()
            for index in range(half // chunk):
                place = pl.ds(pl.multiple_of(y * half + index * chunk, chunk), chunk)
                total = accum[:, place] + product(place).astype(jnp.float32)
                out_ref[own_rows, index * chunk:(index + 1) * chunk] = total
    for index in range(half // chunk):
        last_copy(index).wait_recv()
        part = slice(index * chunk, (index + 1) * chunk)
        out_ref[other_rows, part] = got[:, part].astype(jnp.float32)
    for index in range(half // chunk):
        last_copy(index).wait_send()
    for hops, seg, dz, dx, dy, onward in plan:
        def finish(seg=seg, dz=dz, dx=dx, dy=dy, onward=onward):
            origin = origin_of(dz, dx, dy)
            for move in onward:
                guarded(exists(*move), lambda move=move: copy(seg, origin, move, link_sem).wait_send())
            copy(seg, origin, ("core", 1), side_sem).wait_send()
        guarded(inside(dz), finish)


def series(rows_count, piece, rotation_piece):
    rows, width = piece.shape
    pieces = rows_count * 8
    segs = len(ORDERS)
    vmem = pl.BlockSpec(memory_space=pltpu.VMEM)
    return pl.pallas_call(
        functools.partial(series_kernel, rows_count),
        out_shape=jax.ShapeDtypeStruct((2 * rows, width // 2), jnp.float32),
        in_specs=[vmem, vmem],
        out_specs=vmem,
        scratch_shapes=[
            pltpu.VMEM((width, width), jnp.bfloat16),
            pltpu.VMEM((2, rows, width), jnp.bfloat16),
            pltpu.VMEM((rows, width), jnp.float32),
            pltpu.VMEM((rows, width // 2), jnp.bfloat16),
            pltpu.VMEM((rows, width // 2), jnp.bfloat16),
            pltpu.SemaphoreType.DMA,
            pltpu.SemaphoreType.DMA((segs, pieces)),
            pltpu.SemaphoreType.DMA((segs, pieces)),
            pltpu.SemaphoreType.DMA((segs, 5, pieces)),
            pltpu.SemaphoreType.DMA((width // 1024,)),
            pltpu.SemaphoreType.DMA((width // 1024,)),
        ],
        compiler_params=pltpu.CompilerParams(
            collective_id=3, has_side_effects=True, vmem_limit_bytes=50 * 2**20
        ),
    )(piece, rotation_piece)


def per_device(rows_count, fast, intersection_re, intersection_im, weights, shells, rotation):
    shells_here = intersection_re.shape[0]
    slab_rows = intersection_re.shape[1]
    width = intersection_re.shape[2]
    position = lax.axis_index(("row", "col"))
    layer_index = lax.axis_index("depth")
    depth_count = lax.axis_size("depth")
    block_re = lax.dynamic_slice_in_dim(intersection_re, position * slab_rows, slab_rows, 2)
    block_im = lax.dynamic_slice_in_dim(intersection_im, position * slab_rows, slab_rows, 2)
    diag_piece = jnp.stack(
        [jnp.diagonal(block_re, axis1=1, axis2=2), jnp.diagonal(block_im, axis1=1, axis2=2)], 1
    )
    first_shell = layer_index * shells_here
    own_weights = lax.dynamic_slice_in_dim(weights, first_shell, shells_here, 0)
    own_vectors = (
        lax.dynamic_slice_in_dim(shells, first_shell, shells_here, 0).astype(jnp.float32) * LATTICE
    )
    if fast:
        every = lax.all_gather(diag_piece, ("row", "col", "depth"), axis=0, tiled=False)
        every = every.reshape(-1, depth_count, shells_here, 2, slab_rows)
        every = every.transpose(1, 2, 3, 0, 4).reshape(depth_count * shells_here, 2, width)
        every = every.astype(jnp.float32)
        phases = jnp.arctan2(every[:, 1], every[:, 0])
        vectors = shells.astype(jnp.float32) * LATTICE
        scaled = weights[:, None] * vectors
        centre = -jnp.sum(scaled[:, :, None] * phases[:, None, :], 0)
        own_diag = lax.dynamic_slice_in_dim(every, first_shell, shells_here, 0)
        diag_re = own_diag[:, 0]
        diag_im = own_diag[:, 1]
        phase_own = lax.dynamic_slice_in_dim(phases, first_shell, shells_here, 0)
        spread = phase_own + jnp.sum(own_vectors[:, :, None] * centre[None], 1)
    else:
        diagonals = lax.all_gather(diag_piece, ("row", "col"), axis=2, tiled=True).astype(jnp.float32)
        diag_re = diagonals[:, 0]
        diag_im = diagonals[:, 1]
        phase_own = jnp.arctan2(diag_im, diag_re)
        partial_centre = -jnp.einsum("bk,bn->kn", own_weights[:, None] * own_vectors, phase_own)
        centre = lax.psum(partial_centre, "depth")
        spread = phase_own + jnp.einsum("bk,kn->bn", own_vectors, centre)
    modulus = diag_re * diag_re + diag_im * diag_im
    values_re = intersection_re.astype(jnp.float32)
    values_im = intersection_im.astype(jnp.float32)
    terms = values_re * diag_re[:, None, :] + values_im * diag_im[:, None, :]
    terms = (
        terms
        - spread[:, None, :]
        * (values_im * diag_re[:, None, :] - values_re * diag_im[:, None, :])
        / modulus[:, None, :]
    )
    local_sum = jnp.sum(own_weights[:, None, None] * terms, 0)
    factor = 1.25 / math.sqrt(depth_count * shells_here)
    slab_cols = width // depth_count
    if fast:
        summed = lax.psum_scatter(
            local_sum.astype(jnp.bfloat16), "depth", scatter_dimension=0, tiled=True
        )
        mirrored = lax.all_to_all(
            summed, ("row", "col", "depth"), split_axis=1, concat_axis=0, tiled=True
        )
        anti = (summed.astype(jnp.float32) - mirrored.T.astype(jnp.float32)) * factor
        piece = anti.astype(jnp.bfloat16)
        part = slab_rows // depth_count
        own_rotation = lax.dynamic_slice_in_dim(rotation, layer_index * part, part, 0)
        return series(rows_count, piece, own_rotation)
    mirrored = lax.all_to_all(local_sum, ("row", "col"), split_axis=1, concat_axis=0, tiled=True).T
    operator_rows = (
        lax.psum_scatter(local_sum - mirrored, "depth", scatter_dimension=1, tiled=True) * factor
    )
    operator_piece = operator_rows.astype(jnp.bfloat16)
    operator_cols = lax.all_gather(operator_piece, ("row", "col"), axis=0, tiled=True)
    accum = lax.dynamic_slice_in_dim(rotation, layer_index * slab_cols, slab_cols, 1).astype(
        jnp.float32
    )
    product = jnp.dot(rotation, operator_cols, preferred_element_type=jnp.float32)
    for order in range(1, TERMS):
        series_term = (product / order).astype(jnp.bfloat16)
        accum = accum + series_term.astype(jnp.float32)
        if order + 1 < TERMS:
            piece = lax.all_gather(series_term, "depth", axis=1, tiled=True)
            matching = lax.slice_in_dim(operator_cols, 0, piece.shape[1], axis=0)
            product = jnp.zeros_like(accum) + jnp.dot(
                piece, matching, preferred_element_type=jnp.float32
            )
    return accum


def solution(mesh):
    in_specs = (
        P("depth", ("row", "col"), None),
        P("depth", ("row", "col"), None),
        P(),
        P(),
        P(("row", "col"), None),
    )
    out_specs = P(("row", "col"), "depth")
    rows_count = mesh.shape["row"]
    fast = mesh.shape["col"] == 4 and mesh.shape["depth"] == 2
    return jax.shard_map(
        functools.partial(per_device, rows_count, fast), mesh=mesh, in_specs=in_specs, out_specs=out_specs, check_vma=False
    )
```

```python
import functools
import math

import jax
import jax.numpy as jnp
from jax import lax
from jax.experimental import pallas as pl
from jax.experimental.pallas import tpu as pltpu
from jax.sharding import PartitionSpec as P

TERMS = 8


LATTICE = 0.25


def shift(at, axis, way):
    z, x, y, core = at
    if axis == "z":
        return (z + way, x, y, core)
    if axis == "x":
        return (z, 1 - x, y, core)
    if axis == "y":
        return (z, x, 1 - y, core)
    return (z, x, y, 1 - core)


def device_of(at):
    z, x, y, core = at
    return {"row": z, "col": x * 2 + core, "depth": y}


ORDERS = (("z", "x", "y"), ("x", "y", "z"), ("y", "z", "x"))


def cut(width, parts):
    unit = width // 128
    ends = [unit * i // parts * 128 for i in range(parts + 1)]
    return [(ends[i], ends[i + 1] - ends[i]) for i in range(parts)]


def series_kernel(
    rows_count, piece_ref, rotation_ref, out_ref,
    gen, term, accum, sent, got,
    own_sem, link_sem, side_sem, send_sem, last_send, last_recv,
):
    z = lax.axis_index("row")
    col = lax.axis_index("col")
    y = lax.axis_index("depth")
    x = col // 2
    core = col % 2
    me = (z, x, y, core)
    rows, width = piece_ref.shape
    segments = cut(width, len(ORDERS))

    def exists(axis, way):
        if axis != "z":
            return None
        return z > 0 if way < 0 else z < rows_count - 1

    def guarded(condition, action):
        if condition is None:
            action()
        else:
            pl.when(condition)(action)

    barrier = pltpu.get_barrier_semaphore()
    moves = [("z", -1), ("z", 1), ("x", 1), ("y", 1), ("core", 1)]
    for axis, way in moves:
        def greet(axis=axis, way=way):
            pl.semaphore_signal(
                barrier, inc=1, device_id=device_of(shift(me, axis, way)),
                device_id_type=pl.DeviceIdType.MESH,
            )
        guarded(exists(axis, way), greet)
    peers = 3 + jnp.where(z > 0, 1, 0) + jnp.where(z < rows_count - 1, 1, 0)
    pl.semaphore_wait(barrier, peers)

    def slab(at):
        zo, xo, yo, co = at
        return ((zo * 2 + xo) * 2 + co) * 2 + yo

    own = pltpu.make_async_copy(
        piece_ref, gen.at[pl.ds(pl.multiple_of(slab(me) * rows, rows), rows), :], own_sem
    )
    own.start()
    own.wait()

    def copy(seg, origin, move, recv):
        start, size = segments[seg]
        place = gen.at[
            pl.ds(pl.multiple_of(slab(origin) * rows, rows), rows), pl.ds(start, size)
        ]
        axis, way = move
        return pltpu.make_async_remote_copy(
            src_ref=place, dst_ref=place,
            send_sem=send_sem.at[seg, moves.index(move), slab(origin) % (rows_count * 8)],
            recv_sem=recv.at[seg, slab(origin)],
            device_id=device_of(shift(me, axis, way)),
            device_id_type=pl.DeviceIdType.MESH,
        )

    plan = []
    for dz in range(1 - rows_count, rows_count):
        for dx in range(2):
            for dy in range(2):
                for seg, order in enumerate(ORDERS):
                    offset = {"z": dz, "x": dx, "y": dy}
                    last = max([i for i, a in enumerate(order) if offset[a]], default=-1)
                    onward = []
                    if last >= 0 and order[last] == "z":
                        onward.append(("z", 1 if dz < 0 else -1))
                    for axis in order[last + 1:]:
                        onward += [("z", -1), ("z", 1)] if axis == "z" else [(axis, 1)]
                    plan.append((abs(dz) + dx + dy, seg, dz, dx, dy, onward))
    plan.sort(key=lambda entry: entry[:2])

    def origin_of(dz, dx, dy):
        return (z + dz, 1 - x if dx else x, 1 - y if dy else y, core)

    def inside(dz):
        if dz == 0:
            return None
        return z + dz >= 0 if dz < 0 else z + dz < rows_count

    for hops, seg, dz, dx, dy, onward in plan:
        def handle(hops=hops, seg=seg, dz=dz, dx=dx, dy=dy, onward=onward):
            origin = origin_of(dz, dx, dy)
            if hops:
                copy(seg, origin, ("x", 1), link_sem).wait_recv()
            for move in onward:
                guarded(exists(*move), lambda move=move: copy(seg, origin, move, link_sem).start())
            copy(seg, origin, ("core", 1), side_sem).start()
        guarded(inside(dz), handle)

    for seg in range(len(ORDERS)):
        for zo in range(rows_count):
            for xo in range(2):
                for yo in range(2):
                    copy(seg, (zo, xo, yo, 1 - core), ("core", 1), side_sem).wait_recv()

    chunk = 512
    half = width // 2
    other = device_of(shift(me, "y", 1))

    def last_copy(index):
        place = pl.ds(index * chunk, chunk)
        return pltpu.make_async_remote_copy(
            src_ref=sent.at[:, place], dst_ref=got.at[:, place],
            send_sem=last_send.at[index], recv_sem=last_recv.at[index],
            device_id=other, device_id_type=pl.DeviceIdType.MESH,
        )

    own_rows = pl.ds(pl.multiple_of(y * rows, rows), rows)
    other_rows = pl.ds(pl.multiple_of((1 - y) * rows, rows), rows)
    for order in range(1, TERMS):
        source = rotation_ref if order == 1 else term.at[(order - 1) % 2]

        def product(place):
            value = jnp.dot(source[...], gen[:, place], preferred_element_type=jnp.float32)
            return (value * (1.0 / order)).astype(jnp.bfloat16)

        if order + 1 < TERMS:
            @pl.loop(0, width // chunk)
            def _(index):
                place = pl.ds(pl.multiple_of(index * chunk, chunk), chunk)
                value = product(place)
                term[order % 2, :, place] = value
                base = rotation_ref[:, place].astype(jnp.float32) if order == 1 else accum[:, place]
                accum[:, place] = base + value.astype(jnp.float32)
        else:
            for index in range(half // chunk):
                place = pl.ds(pl.multiple_of((1 - y) * half + index * chunk, chunk), chunk)
                total = accum[:, place] + product(place).astype(jnp.float32)
                sent[:, index * chunk:(index + 1) * chunk] = total.astype(jnp.bfloat16)
                last_copy(index).start()
            for index in range(half // chunk):
                place = pl.ds(pl.multiple_of(y * half + index * chunk, chunk), chunk)
                total = accum[:, place] + product(place).astype(jnp.float32)
                out_ref[own_rows, index * chunk:(index + 1) * chunk] = total
    for index in range(half // chunk):
        last_copy(index).wait_recv()
        part = slice(index * chunk, (index + 1) * chunk)
        out_ref[other_rows, part] = got[:, part].astype(jnp.float32)
    for index in range(half // chunk):
        last_copy(index).wait_send()
    for hops, seg, dz, dx, dy, onward in plan:
        def finish(seg=seg, dz=dz, dx=dx, dy=dy, onward=onward):
            origin = origin_of(dz, dx, dy)
            for move in onward:
                guarded(exists(*move), lambda move=move: copy(seg, origin, move, link_sem).wait_send())
            copy(seg, origin, ("core", 1), side_sem).wait_send()
        guarded(inside(dz), finish)


def series(rows_count, piece, rotation_piece):
    rows, width = piece.shape
    pieces = rows_count * 8
    segs = len(ORDERS)
    vmem = pl.BlockSpec(memory_space=pltpu.VMEM)
    return pl.pallas_call(
        functools.partial(series_kernel, rows_count),
        out_shape=jax.ShapeDtypeStruct((2 * rows, width // 2), jnp.float32),
        in_specs=[vmem, vmem],
        out_specs=vmem,
        scratch_shapes=[
            pltpu.VMEM((width, width), jnp.bfloat16),
            pltpu.VMEM((2, rows, width), jnp.bfloat16),
            pltpu.VMEM((rows, width), jnp.float32),
            pltpu.VMEM((rows, width // 2), jnp.bfloat16),
            pltpu.VMEM((rows, width // 2), jnp.bfloat16),
            pltpu.SemaphoreType.DMA,
            pltpu.SemaphoreType.DMA((segs, pieces)),
            pltpu.SemaphoreType.DMA((segs, pieces)),
            pltpu.SemaphoreType.DMA((segs, 5, pieces)),
            pltpu.SemaphoreType.DMA((width // 1024,)),
            pltpu.SemaphoreType.DMA((width // 1024,)),
        ],
        compiler_params=pltpu.CompilerParams(
            collective_id=3, has_side_effects=True, vmem_limit_bytes=50 * 2**20
        ),
    )(piece, rotation_piece)


def per_device(rows_count, fast, intersection_re, intersection_im, weights, shells, rotation):
    shells_here = intersection_re.shape[0]
    slab_rows = intersection_re.shape[1]
    width = intersection_re.shape[2]
    position = lax.axis_index(("row", "col"))
    layer_index = lax.axis_index("depth")
    depth_count = lax.axis_size("depth")
    block_re = lax.dynamic_slice_in_dim(intersection_re, position * slab_rows, slab_rows, 2)
    block_im = lax.dynamic_slice_in_dim(intersection_im, position * slab_rows, slab_rows, 2)
    diag_piece = jnp.stack(
        [jnp.diagonal(block_re, axis1=1, axis2=2), jnp.diagonal(block_im, axis1=1, axis2=2)], 1
    )
    first_shell = layer_index * shells_here
    own_weights = lax.dynamic_slice_in_dim(weights, first_shell, shells_here, 0)
    own_vectors = (
        lax.dynamic_slice_in_dim(shells, first_shell, shells_here, 0).astype(jnp.float32) * LATTICE
    )
    diagonals = lax.all_gather(diag_piece, ("row", "col"), axis=2, tiled=True).astype(jnp.float32)
    diag_re = diagonals[:, 0]
    diag_im = diagonals[:, 1]
    phase_own = jnp.arctan2(diag_im, diag_re)
    partial_centre = -jnp.einsum("bk,bn->kn", own_weights[:, None] * own_vectors, phase_own)
    centre = lax.psum(partial_centre, "depth")
    spread = phase_own + jnp.einsum("bk,kn->bn", own_vectors, centre)
    modulus = diag_re * diag_re + diag_im * diag_im
    values_re = intersection_re.astype(jnp.float32)
    values_im = intersection_im.astype(jnp.float32)
    terms = values_re * diag_re[:, None, :] + values_im * diag_im[:, None, :]
    terms = (
        terms
        - spread[:, None, :]
        * (values_im * diag_re[:, None, :] - values_re * diag_im[:, None, :])
        / modulus[:, None, :]
    )
    local_sum = jnp.sum(own_weights[:, None, None] * terms, 0)
    factor = 1.25 / math.sqrt(depth_count * shells_here)
    slab_cols = width // depth_count
    if fast:
        summed = lax.psum_scatter(
            local_sum.astype(jnp.bfloat16), "depth", scatter_dimension=0, tiled=True
        )
        mirrored = lax.all_to_all(
            summed, ("row", "col", "depth"), split_axis=1, concat_axis=0, tiled=True
        )
        anti = (summed.astype(jnp.float32) - mirrored.T.astype(jnp.float32)) * factor
        piece = anti.astype(jnp.bfloat16)
        part = slab_rows // depth_count
        own_rotation = lax.dynamic_slice_in_dim(rotation, layer_index * part, part, 0)
        return series(rows_count, piece, own_rotation)
    mirrored = lax.all_to_all(local_sum, ("row", "col"), split_axis=1, concat_axis=0, tiled=True).T
    operator_rows = (
        lax.psum_scatter(local_sum - mirrored, "depth", scatter_dimension=1, tiled=True) * factor
    )
    operator_piece = operator_rows.astype(jnp.bfloat16)
    operator_cols = lax.all_gather(operator_piece, ("row", "col"), axis=0, tiled=True)
    accum = lax.dynamic_slice_in_dim(rotation, layer_index * slab_cols, slab_cols, 1).astype(
        jnp.float32
    )
    product = jnp.dot(rotation, operator_cols, preferred_element_type=jnp.float32)
    for order in range(1, TERMS):
        series_term = (product / order).astype(jnp.bfloat16)
        accum = accum + series_term.astype(jnp.float32)
        if order + 1 < TERMS:
            piece = lax.all_gather(series_term, "depth", axis=1, tiled=True)
            matching = lax.slice_in_dim(operator_cols, 0, piece.shape[1], axis=0)
            product = jnp.zeros_like(accum) + jnp.dot(
                piece, matching, preferred_element_type=jnp.float32
            )
    return accum


def solution(mesh):
    in_specs = (
        P("depth", ("row", "col"), None),
        P("depth", ("row", "col"), None),
        P(),
        P(),
        P(("row", "col"), None),
    )
    out_specs = P(("row", "col"), "depth")
    rows_count = mesh.shape["row"]
    fast = mesh.shape["col"] == 4 and mesh.shape["depth"] == 2
    return jax.shard_map(
        functools.partial(per_device, rows_count, fast), mesh=mesh, in_specs=in_specs, out_specs=out_specs, check_vma=False
    )
```
